32 devices in a mesh: dp: 8 (over z, x), group: 4 (over y, core).
Axes of the slice: x: 2, y: 2, z: 4, core: 2. Of those that a mesh axis runs over, the one named last changes fastest.
Arguments:
- train_grads: float32 [32768, 1024], P(('dp', 'group')), may hold values from -50 to 50
- val_grads: float32 [16, 32, 1024], P('dp', 'group'), may hold values from -6 to 6
- wanted: int32 [8, 8], replicated, may hold values from -1 to 15, as said below
- owner: int32 [8], replicated, may hold values from 0 to 7, each once
Outputs:
- scores: float32 [32768, 256], P(('dp', 'group'))
The draws below stay inside these ranges and needn't reach their ends.
Inputs may be any that keep to these rules, and one draw needn't show every extreme that they name: wanted[b, j] is -1 or the id of a validation block stored on index j of dp, one of j * 2 to j * 2 + 1; training blocks differ in how many slots are used.
All inputs are finite; a program needn't handle non-finite values.
Results may differ from the reference program's by a relative error of at most 0.0003.
Values sent between devices are 32-bit elements; how exact they have to be, the bound alone decides.
A program may use at most 128 MiB of HBM per device.

```python
import math
import jax
import jax.numpy as jnp
from jax import lax

PROJ = 1024
ROWS_DEV = 1024
VAL_DEV = 2
VB = 32
TRAIN = 32768
NVB = 16
N_DP = 8
N_GROUP = 4


def draw_train_grads(key, part):
    key = jax.random.fold_in(key, 3)
    first, second = jax.random.split(key, 2)
    column_scale = jnp.exp(jax.random.uniform(second, (1, PROJ), jnp.float32, math.log(0.3), math.log(3.0)))
    values = jax.random.normal(first, (TRAIN, PROJ), jnp.float32)
    return jnp.clip(values * column_scale, -50.0, 50.0).astype(jnp.float32)


def draw_wanted(key, part):
    key = jax.random.fold_in(key, 7)
    first, second, third = jax.random.split(key, 3)
    threshold = jax.random.randint(first, (N_DP, 1), 300, 1001)
    coin = jax.random.randint(second, (N_DP, N_DP), 0, 1000)
    within = jax.random.randint(third, (N_DP, N_DP), 0, VAL_DEV)
    base = jnp.arange(N_DP, dtype=jnp.int32)[None, :] * VAL_DEV
    return jnp.where(coin < threshold, base + within, -1).astype(jnp.int32)


def level_of(stream_key, extent, cuts, smallest, largest):
    level, own = 1.0, jax.random.fold_in(stream_key, 6)
    for dim, parts in cuts:
        draws = jnp.exp(jax.random.uniform(jax.random.fold_in(own, dim), (parts,), jnp.float32, smallest / len(cuts), largest / len(cuts)))
        level = level * jnp.repeat(draws, extent[dim] // parts).reshape([-1 if axis == dim else 1 for axis in range(len(extent))])
    return level


def centred(stream_key, shape, deviation, bound, cuts=(), kind=jnp.bfloat16):
    factor_of = level_of(stream_key, shape, cuts, -0.22, 0.18) if cuts else 1.0
    entries = jax.random.normal(stream_key, shape, jnp.float32) * deviation * factor_of
    return jnp.minimum(jnp.maximum(entries, -bound), bound).astype(kind)


def setup_inputs(seed: int = 0) -> dict:
    key_of = jax.random.split(jax.random.key(seed), 5)
    train_grads = draw_train_grads(jax.random.fold_in(key_of[4], 71), 0)
    val_grads = centred(key_of[1], (NVB, VB, PROJ), 1.0, 6.0, ((0, 8), (1, 4)), jnp.float32)
    wanted = draw_wanted(jax.random.fold_in(key_of[4], 71), 0)
    owner = jax.random.permutation(key_of[3], N_DP).astype(jnp.int32)
    return dict(train_grads=train_grads, val_grads=val_grads, wanted=wanted, owner=owner)


damping = 0.1

def cholesky_apply(factor, right_side):
    middle = lax.linalg.triangular_solve(factor, right_side, left_side=True, lower=True)
    return lax.linalg.triangular_solve(factor, middle, left_side=True, lower=True, transpose_a=True)

def reference(train_grads, val_grads, wanted, owner):
    highest = lax.Precision.HIGHEST
    gram_matrix = lax.dot_general(train_grads, train_grads, (((0,), (0,)), ((), ())), precision=highest)
    gram_matrix = gram_matrix / TRAIN + damping * jnp.eye(PROJ, dtype=jnp.float32)
    factor = jnp.linalg.cholesky(gram_matrix)
    val_rows = val_grads.reshape(NVB * VB, PROJ)
    solved = cholesky_apply(factor, val_rows.T).T.reshape(NVB, VB, PROJ)
    positions = jnp.arange(N_DP, dtype=jnp.int32)
    holder = jnp.sum(jnp.where(owner[None, :] == positions[:, None], positions[None, :], 0), axis=1).astype(jnp.int32)
    requests = wanted[holder]
    by_block = train_grads.reshape(N_DP, N_GROUP * ROWS_DEV, PROJ)
    score_scale = PROJ ** (-0.5)

    def score_tile(pair):
        block_rows, request = pair
        is_live = (request >= 0).astype(jnp.float32)
        picked = solved[jnp.maximum(request, 0).astype(jnp.int32)] * is_live[:, None, None]
        return lax.dot_general(block_rows, picked.reshape(N_DP * VB, PROJ), (((1,), (1,)), ((), ())), precision=highest) * score_scale
    result = lax.map(score_tile, (by_block, requests))
    return result.reshape(TRAIN, N_DP * VB)
```

```python
import functools

import jax
import jax.numpy as jnp
from jax import lax
from jax.experimental import pallas as pl
from jax.experimental.pallas import tpu as pltpu
from jax.sharding import PartitionSpec as P

damping = 0.1
BLOCK = 128
SUB = 8
highest = lax.Precision.HIGHEST


def invert_block(rows):
    rows = list(rows)
    lane = lax.broadcasted_iota(jnp.int32, (SUB, BLOCK), 1)
    sub = lax.broadcasted_iota(jnp.int32, (SUB, BLOCK), 0)
    is_row = [sub == j for j in range(SUB)]
    for p in range(BLOCK // SUB):
        base = p * SUB
        panel = rows[p]
        cols = [jnp.broadcast_to(panel[:, base + j : base + j + 1], (SUB, BLOCK)) for j in range(SUB)]
        inside = (lane >= base) & (lane < base + SUB)
        new = jnp.where(inside, jnp.where(lane - base == sub, 1.0, 0.0), panel)
        for j in range(SUB):
            inv = 1.0 / cols[j][j : j + 1, :]
            factor = jnp.where(is_row[j], 0.0, cols[j])
            pivot = new[j : j + 1, :] * inv
            for l in range(j + 1, SUB):
                head = cols[l][j : j + 1, :] * inv
                cols[l] = jnp.where(is_row[j], head, cols[l]) - factor * head
            new = jnp.where(is_row[j], pivot, new) - factor * pivot
        for r in range(BLOCK // SUB):
            if r == p:
                continue
            old = rows[r]
            total = jnp.where(inside, 0.0, old)
            for j in range(SUB):
                total = total - old[:, base + j : base + j + 1] * new[j : j + 1, :]
            rows[r] = total
        rows[p] = new
    return rows


def dot(a, b, dims):
    return lax.dot_general(a, b, (dims, ((), ())), precision=highest, preferred_element_type=jnp.float32)


def solve_kernel(rows_total, request, gram, blocks, out, work, upper, diag):
    features = gram.shape[0]
    steps = features // BLOCK
    slots = request.shape[0]
    vb = blocks.shape[1]
    scale = features ** (-0.5)
    for i in range(steps):
        at = pl.ds(i * BLOCK, BLOCK)
        row = lax.broadcasted_iota(jnp.int32, (BLOCK, features), 0) + i * BLOCK
        col = lax.broadcasted_iota(jnp.int32, (BLOCK, features), 1)
        work[at, :] = gram[at, :] / rows_total + jnp.where(row == col, damping, 0.0)

    def pick(j, carry):
        w = request[j]
        live = jnp.where(w >= 0, scale, 0.0).astype(jnp.float32)
        out[pl.ds(pl.multiple_of(j * vb, vb), vb), :] = blocks[jnp.maximum(w, 0)] * live
        return carry

    lax.fori_loop(0, slots, pick, 0)

    def forward(k, carry):
        at = pl.ds(pl.multiple_of(k * BLOCK, BLOCK), BLOCK)
        block = work[at, at]
        inverse = jnp.concatenate(invert_block([block[SUB * r : SUB * r + SUB] for r in range(BLOCK // SUB)]), axis=0)
        diag[at, :] = inverse
        col = lax.broadcasted_iota(jnp.int32, (BLOCK, features), 1)
        panel = jnp.where(col >= (k + 1) * BLOCK, work[at, :], 0.0)
        scaled = dot(inverse, panel, ((1,), (0,)))
        upper[at, :] = scaled
        out[...] -= dot(out[:, at], scaled, ((1,), (0,)))

        def trail(i, carry):
            to = pl.ds(pl.multiple_of(i * BLOCK, BLOCK), BLOCK)
            work[to, :] -= dot(work[at, to], upper[at, :], ((0,), (0,)))
            return carry

        lax.fori_loop(k + 1, steps, trail, 0)
        return carry

    lax.fori_loop(0, steps, forward, 0)

    def backward(i, carry):
        k = steps - 1 - i
        at = pl.ds(pl.multiple_of(k * BLOCK, BLOCK), BLOCK)
        out[:, at] = dot(out[:, at], diag[at, :], ((1,), (0,))) - dot(out[...], upper[at, :], ((1,), (1,)))
        return carry

    lax.fori_loop(0, steps, backward, 0)


def solve(gram_sum, blocks, request, rows_total):
    features = gram_sum.shape[0]
    slots, vb = request.shape[0], blocks.shape[1]
    return pl.pallas_call(
        functools.partial(solve_kernel, rows_total),
        out_shape=jax.ShapeDtypeStruct((slots * vb, features), jnp.float32),
        in_specs=[
            pl.BlockSpec(memory_space=pltpu.SMEM),
            pl.BlockSpec(memory_space=pltpu.VMEM),
            pl.BlockSpec(memory_space=pltpu.VMEM),
        ],
        out_specs=pl.BlockSpec(memory_space=pltpu.VMEM),
        scratch_shapes=[
            pltpu.VMEM((features, features), jnp.float32),
            pltpu.VMEM((features, features), jnp.float32),
            pltpu.VMEM((features, BLOCK), jnp.float32),
        ],
        compiler_params=pltpu.CompilerParams(vmem_limit_bytes=56 * 2**20),
        cost_estimate=pl.CostEstimate(flops=10**10, bytes_accessed=10**7, transcendentals=0),
    )(request, gram_sum, blocks)


def local(train_grads, val_grads, wanted, owner):
    features = train_grads.shape[1]
    devices, group = lax.axis_size("dp"), lax.axis_size("group")
    rows_total = train_grads.shape[0] * devices * group
    gathered = lax.all_gather(val_grads, ("dp", "group"), axis=0, tiled=False)
    per, part = val_grads.shape[0], val_grads.shape[1]
    blocks = gathered.reshape(devices, group, per, part, features).transpose(0, 2, 1, 3, 4)
    blocks = blocks.reshape(devices * per, group * part, features)
    own_index = lax.axis_index("dp")
    mine = jnp.sum(jnp.where(owner == own_index, jnp.arange(devices, dtype=jnp.int32), 0))
    request = lax.dynamic_index_in_dim(wanted, mine, 0, keepdims=False)
    partial_gram = lax.dot_general(train_grads, train_grads, (((0,), (0,)), ((), ())), precision=highest)
    summed = lax.psum(partial_gram, ("dp", "group"))
    solved = solve(summed, blocks, request, rows_total)
    return lax.dot_general(train_grads, solved, (((1,), (1,)), ((), ())), precision=highest)


def solution(mesh):
    in_specs = (P(("dp", "group"), None), P("dp", "group", None), P(), P())
    out_specs = P(("dp", "group"), None)
    return jax.shard_map(local, mesh=mesh, in_specs=in_specs, out_specs=out_specs, check_vma=False)
```

```python
import functools

import jax
import jax.numpy as jnp
from jax import lax
from jax.experimental import pallas as pl
from jax.experimental.pallas import tpu as pltpu
from jax.sharding import PartitionSpec as P

damping = 0.1
BLOCK = 128
SUB = 8
STREAMS = 3
MESH = pl.DeviceIdType.MESH


def upper_blocks(features):
    steps = features // BLOCK
    return [(i, j) for i in range(steps) for j in range(i, steps)]


def sum_plan(dp, group, features):
    rows = len(upper_blocks(features)) * BLOCK
    bits = [("group", 1 << b) for b in range(group.bit_length() - 1)]
    bits += [("dp", 1 << b) for b in range(dp.bit_length() - 1)]
    if (1 << len(bits)) != dp * group or group < 2 or dp < 2:
        return None
    if rows % (STREAMS * SUB * dp * group):
        return None
    first, rest = bits[0], bits[1:]
    turning, last = rest[:-1], rest[-1:]
    count = len(turning)
    streams = [[first] + [turning[(s + t) % count] for t in range(count)] + last for s in range(STREAMS)]
    return streams


def place_of(bit):
    axis, weight = bit
    index = lax.axis_index(axis)
    mine = lax.rem(index // weight, 2)
    return mine, {axis: index + weight * (1 - 2 * mine)}


def sum_kernel(streams, gram, out, total, landed, send_sem, recv_sem):
    features = gram.shape[0]
    rows = total.shape[0]
    depth = len(streams[0])
    bits = sorted(set(streams[0]))
    barrier = pltpu.get_barrier_semaphore()
    for bit in bits:
        pl.semaphore_signal(barrier, inc=1, device_id=place_of(bit)[1], device_id_type=MESH)
    for n, (i, j) in enumerate(upper_blocks(features)):
        total[n * BLOCK : (n + 1) * BLOCK, :] = gram[i * BLOCK : (i + 1) * BLOCK, j * BLOCK : (j + 1) * BLOCK]
    pl.semaphore_wait(barrier, len(bits))

    half = rows // 2
    share = half // STREAMS
    core, sibling = place_of(streams[0][0])

    def at(offset, size):
        return pl.ds(pl.multiple_of(offset, SUB), size)

    held = [[None] * depth for _ in streams]
    away = [[None] * depth for _ in streams]
    slot = [[None] * depth for _ in streams]
    free = 0
    for s, order in enumerate(streams):
        offset, size = core * half + s * share, share
        held[s][0] = (offset, size)
        away[s][0] = ((1 - core) * half + s * share, size)
        for t in range(1, depth):
            mine, _ = place_of(order[t])
            size = size // 2
            away[s][t] = (offset + (1 - mine) * size, size)
            offset = offset + mine * size
            held[s][t] = (offset, size)
        for t in range(depth):
            slot[s][t] = (free, held[s][t][1])
            free += held[s][t][1]

    def out_copy(s, t):
        return pltpu.make_async_remote_copy(
            src_ref=total.at[at(*away[s][t])],
            dst_ref=landed.at[pl.ds(*slot[s][t])],
            send_sem=send_sem.at[0, s, t],
            recv_sem=recv_sem.at[0, s, t],
            device_id=place_of(streams[s][t])[1],
            device_id_type=MESH,
        )

    def back_copy(s, t):
        return pltpu.make_async_remote_copy(
            src_ref=out.at[at(*held[s][t])],
            dst_ref=out.at[at(*held[s][t])],
            send_sem=send_sem.at[1, s, t],
            recv_sem=recv_sem.at[1, s, t],
            device_id=place_of(streams[s][t])[1],
            device_id_type=MESH,
        )

    outs = [[out_copy(s, t) for t in range(depth)] for s in range(len(streams))]
    backs = [[back_copy(s, t) for t in range(depth)] for s in range(len(streams))]
    for s in range(len(streams)):
        outs[s][0].start()
    for t in range(depth):
        for s in range(len(streams)):
            outs[s][t].wait()
            here = at(*held[s][t])
            if t + 1 < depth:
                total[here, :] += landed[pl.ds(*slot[s][t]), :]
                outs[s][t + 1].start()
            else:
                out[here, :] = total[here, :] + landed[pl.ds(*slot[s][t]), :]
                backs[s][t].start()
    for t in reversed(range(depth)):
        for s in range(len(streams)):
            backs[s][t].wait()
            if t > 0:
                backs[s][t - 1].start()


def sum_gram(partial_gram, streams):
    features = partial_gram.shape[0]
    rows = len(upper_blocks(features)) * BLOCK
    depth = len(streams[0])
    return pl.pallas_call(
        functools.partial(sum_kernel, streams),
        out_shape=jax.ShapeDtypeStruct((rows, BLOCK), jnp.float32),
        in_specs=[pl.BlockSpec(memory_space=pltpu.VMEM)],
        out_specs=pl.BlockSpec(memory_space=pltpu.VMEM),
        scratch_shapes=[
            pltpu.VMEM((rows, BLOCK), jnp.float32),
            pltpu.VMEM((rows, BLOCK), jnp.float32),
            pltpu.SemaphoreType.DMA((2, STREAMS, depth)),
            pltpu.SemaphoreType.DMA((2, STREAMS, depth)),
        ],
        compiler_params=pltpu.CompilerParams(
            collective_id=0, has_side_effects=True, vmem_limit_bytes=24 * 2**20
        ),
        cost_estimate=pl.CostEstimate(flops=10**10, bytes_accessed=10**8, transcendentals=0),
    )(partial_gram)


def invert_block(rows):
    rows = list(rows)
    lane = lax.broadcasted_iota(jnp.int32, (SUB, BLOCK), 1)
    sub = lax.broadcasted_iota(jnp.int32, (SUB, BLOCK), 0)
    is_row = [sub == j for j in range(SUB)]
    for p in range(BLOCK // SUB):
        base = p * SUB
        panel = rows[p]
        cols = [jnp.broadcast_to(panel[:, base + j : base + j + 1], (SUB, BLOCK)) for j in range(SUB)]
        inside = (lane >= base) & (lane < base + SUB)
        new = jnp.where(inside, jnp.where(lane - base == sub, 1.0, 0.0), panel)
        for j in range(SUB):
            inv = 1.0 / cols[j][j : j + 1, :]
            factor = jnp.where(is_row[j], 0.0, cols[j])
            pivot = new[j : j + 1, :] * inv
            for l in range(j + 1, SUB):
                head = cols[l][j : j + 1, :] * inv
                cols[l] = jnp.where(is_row[j], head, cols[l]) - factor * head
            new = jnp.where(is_row[j], pivot, new) - factor * pivot
        for r in range(BLOCK // SUB):
            if r == p:
                continue
            old = rows[r]
            total = jnp.where(inside, 0.0, old)
            for j in range(SUB):
                total = total - old[:, base + j : base + j + 1] * new[j : j + 1, :]
            rows[r] = total
        rows[p] = new
    return rows


def halves(x):
    high = x.astype(jnp.bfloat16)
    return high, (x - high.astype(jnp.float32)).astype(jnp.bfloat16)


def dot(a, b):
    a_high, a_low = halves(a)
    b_high, b_low = halves(b)
    left = jnp.concatenate([a_high, a_high, a_low], axis=1)
    right = jnp.concatenate([b_high, b_low, b_high], axis=0)
    return jnp.dot(left, right, preferred_element_type=jnp.float32)


def solve_kernel(rows_total, chunk, request, gram, blocks, out, work, scaled, right):
    features = out.shape[1]
    steps = features // BLOCK
    slots = request.shape[0]
    part = blocks.shape[3]
    vb = blocks.shape[1] * part
    scale = features ** (-0.5)
    diagonal = lax.broadcasted_iota(jnp.int32, (BLOCK, BLOCK), 0) == lax.broadcasted_iota(jnp.int32, (BLOCK, BLOCK), 1)
    for n, (i, j) in enumerate(upper_blocks(features)):
        block = gram[n * BLOCK : (n + 1) * BLOCK, :] / rows_total
        if i == j:
            block = block + jnp.where(diagonal, damping, 0.0)
        else:
            work[j * BLOCK : (j + 1) * BLOCK, i * BLOCK : (i + 1) * BLOCK] = block.T
        work[i * BLOCK : (i + 1) * BLOCK, j * BLOCK : (j + 1) * BLOCK] = block

    def pick(j, carry):
        w = request[j]
        live = jnp.where(w >= 0, scale, 0.0).astype(jnp.float32)
        known = jnp.maximum(w, 0)
        holder, inner = lax.div(known, blocks.shape[2]), lax.rem(known, blocks.shape[2])
        for g in range(blocks.shape[1]):
            to = pl.ds(pl.multiple_of(features + j * vb + g * part, part), part)
            work[to, :] = blocks[holder, g, inner] * live
        return carry

    lax.fori_loop(0, slots, pick, 0)

    def step(k, carry):
        at = pl.ds(pl.multiple_of(k * BLOCK, BLOCK), BLOCK)
        block = work[at, at]
        inverse = jnp.concatenate(invert_block([block[SUB * r : SUB * r + SUB] for r in range(BLOCK // SUB)]), axis=0)
        scaled[...] = inverse
        col = lax.broadcasted_iota(jnp.int32, (BLOCK, features), 1)
        outside = (col < k * BLOCK) | (col >= (k + 1) * BLOCK)
        high, low = halves(jnp.where(outside, work[at, :], 0.0))
        right[0:BLOCK, :] = high
        right[BLOCK : 2 * BLOCK, :] = low
        right[2 * BLOCK :, :] = high

        def update(i, carry):
            to = pl.ds(pl.multiple_of(i * chunk, chunk), chunk)
            column = dot(work[to, at], scaled[...])
            column_high, column_low = halves(column)
            left = jnp.concatenate([column_high, column_high, column_low], axis=1)
            work[to, :] -= jnp.dot(left, right[...], preferred_element_type=jnp.float32)
            work[to, at] = column
            return carry

        lax.fori_loop((k + 1) * BLOCK // chunk, work.shape[0] // chunk, update, 0)
        return carry

    lax.fori_loop(0, steps, step, 0)
    out[...] = work[features:, :]


def solve(gram_sum, blocks, request, rows_total):
    features = blocks.shape[4]
    slots, vb = request.shape[0], blocks.shape[1] * blocks.shape[3]
    chunk = 2 * BLOCK
    return pl.pallas_call(
        functools.partial(solve_kernel, rows_total, chunk),
        out_shape=jax.ShapeDtypeStruct((slots * vb, features), jnp.float32),
        in_specs=[
            pl.BlockSpec(memory_space=pltpu.SMEM),
            pl.BlockSpec(memory_space=pltpu.VMEM),
            pl.BlockSpec(memory_space=pltpu.VMEM),
        ],
        out_specs=pl.BlockSpec(memory_space=pltpu.VMEM),
        scratch_shapes=[
            pltpu.VMEM((features + slots * vb, features), jnp.float32),
            pltpu.VMEM((BLOCK, BLOCK), jnp.float32),
            pltpu.VMEM((3 * BLOCK, features), jnp.bfloat16),
        ],
        compiler_params=pltpu.CompilerParams(vmem_limit_bytes=56 * 2**20),
        cost_estimate=pl.CostEstimate(flops=10**10, bytes_accessed=10**7, transcendentals=0),
    )(request, gram_sum, blocks)


def local(streams, train_grads, val_grads, wanted, owner):
    features = train_grads.shape[1]
    devices, group = lax.axis_size("dp"), lax.axis_size("group")
    rows_total = train_grads.shape[0] * devices * group
    gathered = lax.all_gather(val_grads, ("dp", "group"), axis=0, tiled=False)
    blocks = gathered.reshape((devices, group) + val_grads.shape)
    own_index = lax.axis_index("dp")
    mine = jnp.sum(jnp.where(owner == own_index, jnp.arange(devices, dtype=jnp.int32), 0))
    request = lax.dynamic_index_in_dim(wanted, mine, 0, keepdims=False)
    partial_gram = lax.dot_general(
        train_grads, train_grads, (((0,), (0,)), ((), ())), precision=lax.Precision.HIGH
    )
    if streams is None:
        summed = lax.psum(partial_gram, ("dp", "group"))
        summed = jnp.concatenate(
            [summed[i * BLOCK : (i + 1) * BLOCK, j * BLOCK : (j + 1) * BLOCK] for i, j in upper_blocks(features)]
        )
    else:
        summed = sum_gram(partial_gram, streams)
    solved = solve(summed, blocks, request, rows_total)
    return lax.dot_general(train_grads, solved, (((1,), (1,)), ((), ())), precision=lax.Precision.HIGH)


def solution(mesh):
    in_specs = (P(("dp", "group"), None), P("dp", "group", None), P(), P())
    out_specs = P(("dp", "group"), None)

    def whole(train_grads, val_grads, wanted, owner):
        streams = sum_plan(mesh.shape["dp"], mesh.shape["group"], train_grads.shape[1])
        return jax.shard_map(
            functools.partial(local, streams), mesh=mesh, in_specs=in_specs, out_specs=out_specs, check_vma=False
        )(train_grads, val_grads, wanted, owner)

    return whole
```

```python
import functools

import jax
import jax.numpy as jnp
from jax import lax
from jax.experimental import pallas as pl
from jax.experimental.pallas import tpu as pltpu
from jax.sharding import PartitionSpec as P

damping = 0.1
BLOCK = 128
SUB = 8
STREAMS = 3
GROUPED = 2
MESH = pl.DeviceIdType.MESH


def upper_blocks(features):
    steps = features // BLOCK
    return [(i, j) for i in range(steps) for j in range(i, steps)]


def block_of(strips, i, j):
    strip, row = strips[i // GROUPED], i % GROUPED
    col = j - i // GROUPED * GROUPED
    return strip[row * BLOCK : (row + 1) * BLOCK, col * BLOCK : (col + 1) * BLOCK]


def sum_plan(dp, group, features):
    rows = len(upper_blocks(features)) * BLOCK
    bits = [("group", 1 << b) for b in range(group.bit_length() - 1)]
    bits += [("dp", 1 << b) for b in range(dp.bit_length() - 1)]
    if (1 << len(bits)) != dp * group or group < 2 or dp < 2:
        return None
    if rows % (STREAMS * SUB * dp * group):
        return None
    first, rest = bits[0], bits[1:]
    turning, last = rest[:-1], rest[-1:]
    count = len(turning)
    streams = [[first] + [turning[(s + t) % count] for t in range(count)] + last for s in range(STREAMS)]
    return streams


def place_of(bit):
    axis, weight = bit
    index = lax.axis_index(axis)
    mine = lax.rem(index // weight, 2)
    return mine, {axis: index + weight * (1 - 2 * mine)}


def sum_kernel(streams, *refs):
    *gram, out, total, landed, send_sem, recv_sem = refs
    features = gram[0].shape[1]
    rows = total.shape[0]
    depth = len(streams[0])
    bits = sorted(set(streams[0]))
    barrier = pltpu.get_barrier_semaphore()
    for bit in bits:
        pl.semaphore_signal(barrier, inc=1, device_id=place_of(bit)[1], device_id_type=MESH)
    for n, (i, j) in enumerate(upper_blocks(features)):
        total[n * BLOCK : (n + 1) * BLOCK, :] = block_of(gram, i, j)
    pl.semaphore_wait(barrier, len(bits))

    half = rows // 2
    share = half // STREAMS
    core, sibling = place_of(streams[0][0])

    def at(offset, size):
        return pl.ds(pl.multiple_of(offset, SUB), size)

    held = [[None] * depth for _ in streams]
    away = [[None] * depth for _ in streams]
    slot = [[None] * depth for _ in streams]
    free = 0
    for s, order in enumerate(streams):
        offset, size = core * half + s * share, share
        held[s][0] = (offset, size)
        away[s][0] = ((1 - core) * half + s * share, size)
        for t in range(1, depth):
            mine, _ = place_of(order[t])
            size = size // 2
            away[s][t] = (offset + (1 - mine) * size, size)
            offset = offset + mine * size
            held[s][t] = (offset, size)
        for t in range(depth):
            slot[s][t] = (free, held[s][t][1])
            free += held[s][t][1]

    def out_copy(s, t):
        return pltpu.make_async_remote_copy(
            src_ref=total.at[at(*away[s][t])],
            dst_ref=landed.at[pl.ds(*slot[s][t])],
            send_sem=send_sem.at[0, s, t],
            recv_sem=recv_sem.at[0, s, t],
            device_id=place_of(streams[s][t])[1],
            device_id_type=MESH,
        )

    def back_copy(s, t):
        return pltpu.make_async_remote_copy(
            src_ref=out.at[at(*held[s][t])],
            dst_ref=out.at[at(*held[s][t])],
            send_sem=send_sem.at[1, s, t],
            recv_sem=recv_sem.at[1, s, t],
            device_id=place_of(streams[s][t])[1],
            device_id_type=MESH,
        )

    outs = [[out_copy(s, t) for t in range(depth)] for s in range(len(streams))]
    backs = [[back_copy(s, t) for t in range(depth)] for s in range(len(streams))]
    for s in range(len(streams)):
        outs[s][0].start()
    for t in range(depth):
        for s in range(len(streams)):
            outs[s][t].wait()
            here = at(*held[s][t])
            if t + 1 < depth:
                total[here, :] += landed[pl.ds(*slot[s][t]), :]
                outs[s][t + 1].start()
            else:
                out[here, :] = total[here, :] + landed[pl.ds(*slot[s][t]), :]
                backs[s][t].start()
    for t in reversed(range(depth)):
        for s in range(len(streams)):
            backs[s][t].wait()
            if t > 0:
                backs[s][t - 1].start()


def sum_gram(strips, streams):
    features = strips[0].shape[1]
    rows = len(upper_blocks(features)) * BLOCK
    depth = len(streams[0])
    return pl.pallas_call(
        functools.partial(sum_kernel, streams),
        out_shape=jax.ShapeDtypeStruct((rows, BLOCK), jnp.float32),
        in_specs=[pl.BlockSpec(memory_space=pltpu.VMEM)] * len(strips),
        out_specs=pl.BlockSpec(memory_space=pltpu.VMEM),
        scratch_shapes=[
            pltpu.VMEM((rows, BLOCK), jnp.float32),
            pltpu.VMEM((rows, BLOCK), jnp.float32),
            pltpu.SemaphoreType.DMA((2, STREAMS, depth)),
            pltpu.SemaphoreType.DMA((2, STREAMS, depth)),
        ],
        compiler_params=pltpu.CompilerParams(
            collective_id=0, has_side_effects=True, vmem_limit_bytes=24 * 2**20
        ),
        cost_estimate=pl.CostEstimate(flops=10**10, bytes_accessed=10**8, transcendentals=0),
    )(*strips)


def reciprocal(x):
    guess = pl.reciprocal(x, approx=True)
    for _ in range(2):
        guess = guess * (2.0 - x * guess)
    return guess


def invert_block(rows):
    rows = list(rows)
    lane = lax.broadcasted_iota(jnp.int32, (SUB, BLOCK), 1)
    sub = lax.broadcasted_iota(jnp.int32, (SUB, BLOCK), 0)
    is_row = [sub == j for j in range(SUB)]
    for p in range(BLOCK // SUB):
        base = p * SUB
        panel = rows[p]
        cols = [jnp.broadcast_to(panel[:, base + j : base + j + 1], (SUB, BLOCK)) for j in range(SUB)]
        inside = (lane >= base) & (lane < base + SUB)
        new = jnp.where(inside, jnp.where(lane - base == sub, 1.0, 0.0), panel)
        for j in range(0, SUB, 2):
            one, two = is_row[j], is_row[j + 1]
            both = one | two
            first, second = cols[j], cols[j + 1]
            aa, ab, bb = first[j : j + 1, :], second[j : j + 1, :], second[j + 1 : j + 2, :]
            inv = reciprocal(aa * bb - ab * ab)
            first, second = jnp.where(both, 0.0, first), jnp.where(both, 0.0, second)

            def eliminate(x):
                top, low = x[j : j + 1, :], x[j + 1 : j + 2, :]
                top, low = (bb * top - ab * low) * inv, (aa * low - ab * top) * inv
                kept = jnp.where(one, top, jnp.where(two, low, x))
                return kept - (first * top + second * low)

            for l in range(j + 2, SUB):
                cols[l] = eliminate(cols[l])
            new = eliminate(new)
        for step in range(1, BLOCK // SUB):
            r = (p + step) % (BLOCK // SUB)
            old = rows[r]
            terms = [old[:, base + j : base + j + 1] * new[j : j + 1, :] for j in range(SUB)]
            while len(terms) > 1:
                terms = [x + y for x, y in zip(terms[::2], terms[1::2])]
            rows[r] = jnp.where(inside, 0.0, old) - terms[0]
        rows[p] = new
    return rows


def halves(x):
    high = x.astype(jnp.bfloat16)
    return high, (x - high.astype(jnp.float32)).astype(jnp.bfloat16)


def dot(a, b):
    a_high, a_low = halves(a)
    b_high, b_low = halves(b)
    left = jnp.concatenate([a_high, a_high, a_low], axis=1)
    right = jnp.concatenate([b_high, b_low, b_high], axis=0)
    return jnp.dot(left, right, preferred_element_type=jnp.float32)


def solve_kernel(rows_total, chunk, request, gram, blocks, out, work, scaled, right):
    features = out.shape[1]
    steps = features // BLOCK
    slots = request.shape[0]
    part = blocks.shape[3]
    vb = blocks.shape[1] * part
    scale = features ** (-0.5)
    diagonal = lax.broadcasted_iota(jnp.int32, (BLOCK, BLOCK), 0) == lax.broadcasted_iota(jnp.int32, (BLOCK, BLOCK), 1)
    for n, (i, j) in enumerate(upper_blocks(features)):
        block = gram[n * BLOCK : (n + 1) * BLOCK, :] / rows_total
        if i == j:
            block = block + jnp.where(diagonal, damping, 0.0)
        else:
            work[j * BLOCK : (j + 1) * BLOCK, i * BLOCK : (i + 1) * BLOCK] = block.T
        work[i * BLOCK : (i + 1) * BLOCK, j * BLOCK : (j + 1) * BLOCK] = block

    def pick(j, carry):
        w = request[j]
        live = jnp.where(w >= 0, scale, 0.0).astype(jnp.float32)
        known = jnp.maximum(w, 0)
        holder, inner = lax.div(known, blocks.shape[2]), lax.rem(known, blocks.shape[2])
        for g in range(blocks.shape[1]):
            to = pl.ds(pl.multiple_of(features + j * vb + g * part, part), part)
            work[to, :] = blocks[holder, g, inner] * live
        return carry

    lax.fori_loop(0, slots, pick, 0)

    def step(k, carry):
        at = pl.ds(pl.multiple_of(k * BLOCK, BLOCK), BLOCK)
        block = work[at, at]
        inverse = jnp.concatenate(invert_block([block[SUB * r : SUB * r + SUB] for r in range(BLOCK // SUB)]), axis=0)
        col = lax.broadcasted_iota(jnp.int32, (BLOCK, features), 1)
        outside = (col < k * BLOCK) | (col >= (k + 1) * BLOCK)
        scaled[...] = dot(inverse, jnp.where(outside, work[at, :], 0.0))
        scaled[:, at] = -inverse
        high, low = halves(scaled[...])
        right[0:BLOCK, :] = high
        right[BLOCK : 2 * BLOCK, :] = low
        right[2 * BLOCK :, :] = high

        def update(i, carry):
            to = pl.ds(pl.multiple_of(i * chunk, chunk), chunk)
            high, low = halves(work[to, at])
            left = jnp.concatenate([high, high, low], axis=1)
            work[to, at] = jnp.zeros((chunk, BLOCK), jnp.float32)
            work[to, :] -= jnp.dot(left, right[...], preferred_element_type=jnp.float32)
            return carry

        lax.fori_loop((k + 1) * BLOCK // chunk, work.shape[0] // chunk, update, 0)
        return carry

    lax.fori_loop(0, steps, step, 0)
    out[...] = work[features:, :]


def solve(gram_sum, blocks, request, rows_total):
    features = blocks.shape[4]
    slots, vb = request.shape[0], blocks.shape[1] * blocks.shape[3]
    chunk = 2 * BLOCK
    return pl.pallas_call(
        functools.partial(solve_kernel, rows_total, chunk),
        out_shape=jax.ShapeDtypeStruct((slots * vb, features), jnp.float32),
        in_specs=[
            pl.BlockSpec(memory_space=pltpu.SMEM),
            pl.BlockSpec(memory_space=pltpu.VMEM),
            pl.BlockSpec(memory_space=pltpu.VMEM),
        ],
        out_specs=pl.BlockSpec(memory_space=pltpu.VMEM),
        scratch_shapes=[
            pltpu.VMEM((features + slots * vb, features), jnp.float32),
            pltpu.VMEM((BLOCK, features), jnp.float32),
            pltpu.VMEM((3 * BLOCK, features), jnp.bfloat16),
        ],
        compiler_params=pltpu.CompilerParams(vmem_limit_bytes=56 * 2**20),
        cost_estimate=pl.CostEstimate(flops=10**10, bytes_accessed=10**7, transcendentals=0),
    )(request, gram_sum, blocks)


def local(streams, train_grads, val_grads, wanted, owner):
    features = train_grads.shape[1]
    devices, group = lax.axis_size("dp"), lax.axis_size("group")
    rows_total = train_grads.shape[0] * devices * group
    gathered = lax.all_gather(val_grads, ("dp", "group"), axis=0, tiled=False)
    blocks = gathered.reshape((devices, group) + val_grads.shape)
    own_index = lax.axis_index("dp")
    mine = jnp.sum(jnp.where(owner == own_index, jnp.arange(devices, dtype=jnp.int32), 0))
    request = lax.dynamic_index_in_dim(wanted, mine, 0, keepdims=False)
    strip = GROUPED * BLOCK
    strips = [
        lax.dot_general(
            train_grads[:, start : start + strip],
            train_grads[:, start:],
            (((0,), (0,)), ((), ())),
            precision=lax.Precision.HIGH,
        )
        for start in range(0, features, strip)
    ]
    if streams is None:
        strips = lax.psum(strips, ("dp", "group"))
        summed = jnp.concatenate([block_of(strips, i, j) for i, j in upper_blocks(features)])
    else:
        summed = sum_gram(strips, streams)
    solved = solve(summed, blocks, request, rows_total)
    return lax.dot_general(train_grads, solved, (((1,), (1,)), ((), ())), precision=lax.Precision.HIGH)


def solution(mesh):
    in_specs = (P(("dp", "group"), None), P("dp", "group", None), P(), P())
    out_specs = P(("dp", "group"), None)

    def whole(train_grads, val_grads, wanted, owner):
        streams = sum_plan(mesh.shape["dp"], mesh.shape["group"], train_grads.shape[1])
        return jax.shard_map(
            functools.partial(local, streams), mesh=mesh, in_specs=in_specs, out_specs=out_specs, check_vma=False
        )(train_grads, val_grads, wanted, owner)

    return whole
```

```python
import functools

import jax
import jax.numpy as jnp
from jax import lax
from jax.experimental import pallas as pl
from jax.experimental.pallas import tpu as pltpu
from jax.sharding import PartitionSpec as P

damping = 0.1
BLOCK = 128
SUB = 8
STREAMS = 3
GROUPED = 2
MESH = pl.DeviceIdType.MESH


def upper_blocks(features):
    steps = features // BLOCK
    return [(i, j) for i in range(steps) for j in range(i, steps)]


def block_of(strips, i, j):
    strip, row = strips[i // GROUPED], i % GROUPED
    col = j - i // GROUPED * GROUPED
    return strip[row * BLOCK : (row + 1) * BLOCK, col * BLOCK : (col + 1) * BLOCK]


def sum_plan(dp, group, features):
    rows = len(upper_blocks(features)) * BLOCK
    bits = [("group", 1 << b) for b in range(group.bit_length() - 1)]
    bits += [("dp", 1 << b) for b in range(dp.bit_length() - 1)]
    if (1 << len(bits)) != dp * group or group < 2 or dp < 2:
        return None
    if rows % (STREAMS * SUB * dp * group):
        return None
    first, rest = bits[0], bits[1:]
    turning, last = rest[:-1], rest[-1:]
    count = len(turning)
    streams = [[first] + [turning[(s + t) % count] for t in range(count)] + last for s in range(STREAMS)]
    return streams


def place_of(bit):
    axis, weight = bit
    index = lax.axis_index(axis)
    mine = lax.rem(index // weight, 2)
    return mine, {axis: index + weight * (1 - 2 * mine)}


def sum_kernel(streams, *refs):
    own, *gram, out, vals, total, landed, send_sem, recv_sem, val_send, val_recv = refs
    features = gram[0].shape[1]
    rows = total.shape[0]
    depth = len(streams[0])
    bits = sorted(set(streams[0]))
    barrier = pltpu.get_barrier_semaphore()
    for bit in bits:
        pl.semaphore_signal(barrier, inc=1, device_id=place_of(bit)[1], device_id_type=MESH)
    val_held, place, span = [], 0, vals.shape[0]
    for bit in streams[0]:
        span = span // 2
        place = place + place_of(bit)[0] * span
        val_held.append((place, span))
    vals[pl.ds(place, 1)] = own[...][None]

    def val_copy(t):
        return pltpu.make_async_remote_copy(
            src_ref=vals.at[pl.ds(*val_held[t])],
            dst_ref=vals.at[pl.ds(*val_held[t])],
            send_sem=val_send.at[t],
            recv_sem=val_recv.at[t],
            device_id=place_of(streams[0][t])[1],
            device_id_type=MESH,
        )

    val_copies = [val_copy(t) for t in reversed(range(depth))]
    val_waits = (1, 2, 4, 6)
    for n, (i, j) in enumerate(upper_blocks(features)):
        total[n * BLOCK : (n + 1) * BLOCK, :] = block_of(gram, i, j)
    pl.semaphore_wait(barrier, len(bits))

    half = rows // 2
    share = half // STREAMS
    core, sibling = place_of(streams[0][0])

    def at(offset, size):
        return pl.ds(pl.multiple_of(offset, SUB), size)

    held = [[None] * depth for _ in streams]
    away = [[None] * depth for _ in streams]
    slot = [[None] * depth for _ in streams]
    free = 0
    for s, order in enumerate(streams):
        offset, size = core * half + s * share, share
        held[s][0] = (offset, size)
        away[s][0] = ((1 - core) * half + s * share, size)
        for t in range(1, depth):
            mine, _ = place_of(order[t])
            size = size // 2
            away[s][t] = (offset + (1 - mine) * size, size)
            offset = offset + mine * size
            held[s][t] = (offset, size)
        for t in range(depth):
            slot[s][t] = (free, held[s][t][1])
            free += held[s][t][1]

    def out_copy(s, t):
        return pltpu.make_async_remote_copy(
            src_ref=total.at[at(*away[s][t])],
            dst_ref=landed.at[pl.ds(*slot[s][t])],
            send_sem=send_sem.at[0, s, t],
            recv_sem=recv_sem.at[0, s, t],
            device_id=place_of(streams[s][t])[1],
            device_id_type=MESH,
        )

    def back_copy(s, t):
        return pltpu.make_async_remote_copy(
            src_ref=out.at[at(*held[s][t])],
            dst_ref=out.at[at(*held[s][t])],
            send_sem=send_sem.at[1, s, t],
            recv_sem=recv_sem.at[1, s, t],
            device_id=place_of(streams[s][t])[1],
            device_id_type=MESH,
        )

    outs = [[out_copy(s, t) for t in range(depth)] for s in range(len(streams))]
    backs = [[back_copy(s, t) for t in range(depth)] for s in range(len(streams))]
    for s in range(len(streams)):
        outs[s][0].start()
    val_copies[0].start()
    val_done = 0
    for t in range(depth):
        for s in range(len(streams)):
            outs[s][t].wait()
            here = at(*held[s][t])
            if t + 1 < depth:
                total[here, :] += landed[pl.ds(*slot[s][t]), :]
                outs[s][t + 1].start()
            else:
                out[here, :] = total[here, :] + landed[pl.ds(*slot[s][t]), :]
                backs[s][t].start()
        if t in val_waits and val_done + 1 < depth:
            val_copies[val_done].wait()
            val_done += 1
            val_copies[val_done].start()
    for t in reversed(range(depth)):
        for s in range(len(streams)):
            backs[s][t].wait()
            if t > 0:
                backs[s][t - 1].start()
        if 2 * depth - 1 - t in val_waits and val_done + 1 < depth:
            val_copies[val_done].wait()
            val_done += 1
            val_copies[val_done].start()
    while val_done < depth:
        val_copies[val_done].wait()
        val_done += 1
        if val_done < depth:
            val_copies[val_done].start()


def sum_gram(val_grads, strips, streams):
    features = strips[0].shape[1]
    rows = len(upper_blocks(features)) * BLOCK
    depth = len(streams[0])
    return pl.pallas_call(
        functools.partial(sum_kernel, streams),
        out_shape=[
            jax.ShapeDtypeStruct((rows, BLOCK), jnp.float32),
            jax.ShapeDtypeStruct((1 << depth,) + val_grads.shape, jnp.float32),
        ],
        in_specs=[pl.BlockSpec(memory_space=pltpu.VMEM)] * (1 + len(strips)),
        out_specs=[pl.BlockSpec(memory_space=pltpu.VMEM)] * 2,
        scratch_shapes=[
            pltpu.VMEM((rows, BLOCK), jnp.float32),
            pltpu.VMEM((rows, BLOCK), jnp.float32),
            pltpu.SemaphoreType.DMA((2, STREAMS, depth)),
            pltpu.SemaphoreType.DMA((2, STREAMS, depth)),
            pltpu.SemaphoreType.DMA((depth,)),
            pltpu.SemaphoreType.DMA((depth,)),
        ],
        compiler_params=pltpu.CompilerParams(
            collective_id=0, has_side_effects=True, vmem_limit_bytes=24 * 2**20
        ),
        cost_estimate=pl.CostEstimate(flops=10**10, bytes_accessed=10**8, transcendentals=0),
    )(val_grads, *strips)


def reciprocal(x):
    guess = pl.reciprocal(x, approx=True)
    for _ in range(2):
        guess = guess * (2.0 - x * guess)
    return guess


def invert_block(rows):
    rows = list(rows)
    lane = lax.broadcasted_iota(jnp.int32, (SUB, BLOCK), 1)
    sub = lax.broadcasted_iota(jnp.int32, (SUB, BLOCK), 0)
    is_row = [sub == j for j in range(SUB)]
    for p in range(BLOCK // SUB):
        base = p * SUB
        panel = rows[p]
        cols = [jnp.broadcast_to(panel[:, base + j : base + j + 1], (SUB, BLOCK)) for j in range(SUB)]
        inside = (lane >= base) & (lane < base + SUB)
        new = jnp.where(inside, jnp.where(lane - base == sub, 1.0, 0.0), panel)
        for j in range(0, SUB, 2):
            one, two = is_row[j], is_row[j + 1]
            both = one | two
            first, second = cols[j], cols[j + 1]
            aa, ab, bb = first[j : j + 1, :], second[j : j + 1, :], second[j + 1 : j + 2, :]
            inv = reciprocal(aa * bb - ab * ab)
            first, second = jnp.where(both, 0.0, first), jnp.where(both, 0.0, second)

            def eliminate(x):
                top, low = x[j : j + 1, :], x[j + 1 : j + 2, :]
                top, low = (bb * top - ab * low) * inv, (aa * low - ab * top) * inv
                kept = jnp.where(one, top, jnp.where(two, low, x))
                return kept - (first * top + second * low)

            for l in range(j + 2, SUB):
                cols[l] = eliminate(cols[l])
            new = eliminate(new)
        for step in range(1, BLOCK // SUB):
            r = (p + step) % (BLOCK // SUB)
            old = rows[r]
            terms = [old[:, base + j : base + j + 1] * new[j : j + 1, :] for j in range(SUB)]
            while len(terms) > 1:
                terms = [x + y for x, y in zip(terms[::2], terms[1::2])]
            rows[r] = jnp.where(inside, 0.0, old) - terms[0]
        rows[p] = new
    return rows


def halves(x):
    high = x.astype(jnp.bfloat16)
    return high, (x - high.astype(jnp.float32)).astype(jnp.bfloat16)


def dot(a, b):
    a_high, a_low = halves(a)
    b_high, b_low = halves(b)
    left = jnp.concatenate([a_high, a_high, a_low], axis=1)
    right = jnp.concatenate([b_high, b_low, b_high], axis=0)
    return jnp.dot(left, right, preferred_element_type=jnp.float32)


def piece_of(d, g, group, order):
    if order is None:
        return d * group + g
    place = 0
    for axis, weight in order:
        place = 2 * place + (g // weight % 2 if axis == "group" else lax.rem(lax.div(d, weight), 2))
    return place


def solve_kernel(rows_total, chunk, order, group, request, gram, blocks, out, work, scaled, right):
    features = out.shape[1]
    steps = features // BLOCK
    slots = request.shape[0]
    per, part = blocks.shape[1], blocks.shape[2]
    vb = group * part
    scale = features ** (-0.5)
    diagonal = lax.broadcasted_iota(jnp.int32, (BLOCK, BLOCK), 0) == lax.broadcasted_iota(jnp.int32, (BLOCK, BLOCK), 1)
    for n, (i, j) in enumerate(upper_blocks(features)):
        block = gram[n * BLOCK : (n + 1) * BLOCK, :] / rows_total
        if i == j:
            block = block + jnp.where(diagonal, damping, 0.0)
        else:
            work[j * BLOCK : (j + 1) * BLOCK, i * BLOCK : (i + 1) * BLOCK] = block.T
        work[i * BLOCK : (i + 1) * BLOCK, j * BLOCK : (j + 1) * BLOCK] = block

    def pick(j, carry):
        w = request[j]
        live = jnp.where(w >= 0, scale, 0.0).astype(jnp.float32)
        known = jnp.maximum(w, 0)
        holder, inner = lax.div(known, per), lax.rem(known, per)
        for g in range(group):
            to = pl.ds(pl.multiple_of(features + j * vb + g * part, part), part)
            work[to, :] = blocks[piece_of(holder, g, group, order), inner] * live
        return carry

    lax.fori_loop(0, slots, pick, 0)

    def step(k, carry):
        at = pl.ds(pl.multiple_of(k * BLOCK, BLOCK), BLOCK)
        block = work[at, at]
        inverse = jnp.concatenate(invert_block([block[SUB * r : SUB * r + SUB] for r in range(BLOCK // SUB)]), axis=0)
        col = lax.broadcasted_iota(jnp.int32, (BLOCK, features), 1)
        outside = (col < k * BLOCK) | (col >= (k + 1) * BLOCK)
        scaled[...] = dot(inverse, jnp.where(outside, work[at, :], 0.0))
        scaled[:, at] = -inverse
        high, low = halves(scaled[...])
        right[0:BLOCK, :] = high
        right[BLOCK : 2 * BLOCK, :] = low
        right[2 * BLOCK :, :] = high

        def update(i, carry):
            to = pl.ds(pl.multiple_of(i * chunk, chunk), chunk)
            high, low = halves(work[to, at])
            left = jnp.concatenate([high, high, low], axis=1)
            work[to, at] = jnp.zeros((chunk, BLOCK), jnp.float32)
            work[to, :] -= jnp.dot(left, right[...], preferred_element_type=jnp.float32)
            return carry

        lax.fori_loop((k + 1) * BLOCK // chunk, work.shape[0] // chunk, update, 0)
        return carry

    lax.fori_loop(0, steps, step, 0)
    out[...] = work[features:, :]


def solve(gram_sum, blocks, request, rows_total, order, group):
    features = blocks.shape[3]
    slots, vb = request.shape[0], group * blocks.shape[2]
    chunk = 2 * BLOCK
    return pl.pallas_call(
        functools.partial(solve_kernel, rows_total, chunk, order, group),
        out_shape=jax.ShapeDtypeStruct((slots * vb, features), jnp.float32),
        in_specs=[
            pl.BlockSpec(memory_space=pltpu.SMEM),
            pl.BlockSpec(memory_space=pltpu.VMEM),
            pl.BlockSpec(memory_space=pltpu.VMEM),
        ],
        out_specs=pl.BlockSpec(memory_space=pltpu.VMEM),
        scratch_shapes=[
            pltpu.VMEM((features + slots * vb, features), jnp.float32),
            pltpu.VMEM((BLOCK, features), jnp.float32),
            pltpu.VMEM((3 * BLOCK, features), jnp.bfloat16),
        ],
        compiler_params=pltpu.CompilerParams(vmem_limit_bytes=56 * 2**20),
        cost_estimate=pl.CostEstimate(flops=10**10, bytes_accessed=10**7, transcendentals=0),
    )(request, gram_sum, blocks)


def local(streams, train_grads, val_grads, wanted, owner):
    features = train_grads.shape[1]
    devices, group = lax.axis_size("dp"), lax.axis_size("group")
    rows_total = train_grads.shape[0] * devices * group
    own_index = lax.axis_index("dp")
    mine = jnp.sum(jnp.where(owner == own_index, jnp.arange(devices, dtype=jnp.int32), 0))
    request = lax.dynamic_index_in_dim(wanted, mine, 0, keepdims=False)
    strip = GROUPED * BLOCK
    strips = [
        lax.dot_general(
            train_grads[:, start : start + strip],
            train_grads[:, start:],
            (((0,), (0,)), ((), ())),
            precision=lax.Precision.HIGH,
        )
        for start in range(0, features, strip)
    ]
    if streams is None:
        order = None
        blocks = lax.all_gather(val_grads, ("dp", "group"), axis=0, tiled=False)
        strips = lax.psum(strips, ("dp", "group"))
        summed = jnp.concatenate([block_of(strips, i, j) for i, j in upper_blocks(features)])
    else:
        order = streams[0]
        summed, blocks = sum_gram(val_grads, strips, streams)
    solved = solve(summed, blocks, request, rows_total, order, group)
    return lax.dot_general(train_grads, solved, (((1,), (1,)), ((), ())), precision=lax.Precision.HIGH)


def solution(mesh):
    in_specs = (P(("dp", "group"), None), P("dp", "group", None), P(), P())
    out_specs = P(("dp", "group"), None)

    def whole(train_grads, val_grads, wanted, owner):
        streams = sum_plan(mesh.shape["dp"], mesh.shape["group"], train_grads.shape[1])
        return jax.shard_map(
            functools.partial(local, streams), mesh=mesh, in_specs=in_specs, out_specs=out_specs, check_vma=False
        )(train_grads, val_grads, wanted, owner)

    return whole
```
